512 devices in a mesh: seq: 128 (over z, x, y_hi), dp: 4 (over y_lo, core).
Axes of the slice: x: 4, y: 8 (y_hi: 4, y_lo: 2; y = y_hi * 2 + y_lo), z: 8, core: 2. Of those that a mesh axis runs over, the one named last changes fastest.
Arguments:
- q_raw: bfloat16 [4, 16384, 2560], P('dp', 'seq'), may hold values from -40 to 40
- k_raw: bfloat16 [4, 16384, 2560], P('dp', 'seq'), may hold values from -40 to 40
- values: bfloat16 [4, 16384, 2560], P('dp', 'seq'), may hold values from -6 to 6
- d_attn: bfloat16 [4, 16384, 2560], P('dp', 'seq'), may hold values from -180 to 180
- q_gain: float32 [2560], replicated, may hold values from 0.5 to 1.5
- k_gain: float32 [2560], replicated, may hold values from 0.5 to 1.5
- kv_lists: int32 [128, 5], P('seq'), may hold values from -1 to 127, as said below
Outputs:
- d_q_raw: bfloat16 [4, 16384, 2560], P('dp', 'seq')
- d_k_raw: bfloat16 [4, 16384, 2560], P('dp', 'seq')
- d_values: bfloat16 [4, 16384, 2560], P('dp', 'seq')
- d_q_gain: float32 [2560], replicated
- d_k_gain: float32 [2560], replicated
The draws below stay inside these ranges and needn't reach their ends.
Inputs may be any that keep to these rules, and one draw needn't show every extreme that they name: `kv_lists`: row b serves query block b. Slot 0 holds b; for l below 2, slot 2l+1 holds b - 2^l or -1 and slot 2l+2 holds b + 2^l or -1; a slot is -1 whenever its block would lie outside the video, and any slot other than slot 0 may also be -1 because an earlier pruning step dropped that key block.
All inputs are finite; a program needn't handle non-finite values.
Results may differ from the reference program's by a relative error of at most 0.022.
Values may be sent and summed in bfloat16 or wider, within the bound.
A program may use at most 128 MiB of HBM per device.

```python
import math
from functools import reduce
import jax
import jax.numpy as jnp
from jax import lax

HEADS = 20
HEAD_DIM = 128
BLOCK = 128
LEVELS = 2
BLK_DEV = 1
WIDTH = 2560
SEQ_LEN = 16384
QBLOCKS = 128
VIDEOS = 4


def log_scales(key, scale_shape, spread):
    return jnp.exp((jax.random.uniform(key, scale_shape) - 0.5) * math.log(spread))


def draw_q_raw(key, part):
    key = jax.random.fold_in(key, 21)
    row_key, col_key, val_key = jax.random.split(key, 3)
    field_shape = (VIDEOS, SEQ_LEN, WIDTH)
    base_field = jnp.clip(jax.random.normal(val_key, field_shape), -4.0, 4.0)
    spread = 10.0
    drawn_field = base_field * log_scales(row_key, (VIDEOS, SEQ_LEN, 1), spread) * log_scales(col_key, (1, 1, WIDTH), spread)
    return drawn_field.astype(jnp.bfloat16)


def draw_k_raw(key, part):
    key = jax.random.fold_in(key, 22)
    row_key, col_key, val_key = jax.random.split(key, 3)
    field_shape = (VIDEOS, SEQ_LEN, WIDTH)
    base_field = jnp.clip(jax.random.normal(val_key, field_shape), -4.0, 4.0)
    spread = 10.0
    drawn_field = base_field * log_scales(row_key, (VIDEOS, SEQ_LEN, 1), spread) * log_scales(col_key, (1, 1, WIDTH), spread)
    return drawn_field.astype(jnp.bfloat16)


def draw_d_attn(key, part):
    key = jax.random.fold_in(key, 41)
    val_key = jax.random.fold_in(key, 0)
    field_shape = (VIDEOS, SEQ_LEN, WIDTH)
    position = jnp.arange(SEQ_LEN, dtype=jnp.float32)
    growth = jnp.exp(position / SEQ_LEN * math.log(3.0))
    base_field = jnp.clip(jax.random.normal(val_key, field_shape), -4.0, 4.0)
    return (4.0 * base_field * growth[None, :, None]).astype(jnp.bfloat16)


def draw_kv_lists(key, part):
    key = jax.random.fold_in(key, 11)
    offset_table = [0]
    limit_table = [10]
    for stride_exp in range(LEVELS):
        offset_table = offset_table + [-2 ** stride_exp, 2 ** stride_exp]
        limit_table = limit_table + [max(9 - 2 * stride_exp, 3), max(9 - 2 * stride_exp, 3)]
    offsets = jnp.array(offset_table, jnp.int32)
    keep_limit = jnp.array(limit_table, jnp.int32)
    dice_rolls = jax.random.randint(key, (QBLOCKS, len(offset_table)), 0, 10)
    row_index = jnp.arange(QBLOCKS, dtype=jnp.int32)[:, None]
    target = row_index + offsets[None, :] * BLK_DEV
    kept_mask = (dice_rolls < keep_limit[None, :]) & (target >= 0) & (target < QBLOCKS)
    return jnp.where(kept_mask, target, -1).astype(jnp.int32)


def block_scale(rng, dims, cuts, low, high):
    level = 1.0
    for dim, parts in cuts:
        heights = jax.random.uniform(jax.random.fold_in(jax.random.fold_in(rng, 6), dim), (parts,), jnp.float32, low / len(cuts), high / len(cuts))
        level = level * jnp.repeat(jnp.exp(heights), dims[dim] // parts).reshape((-1,) + (1,) * (len(dims) - 1 - dim))
    return level


def bell_draw(own_key, extent, deviation, most, shards=(), held_as=jnp.bfloat16):
    gain = block_scale(own_key, extent, shards, -0.22, 0.18) if shards else 1.0
    values = jax.random.normal(own_key, extent, jnp.float32) * deviation * gain
    return jnp.minimum(jnp.maximum(values, -most), most).astype(held_as)


def setup_inputs(seed: int = 0) -> dict:
    key_list = jax.random.split(jax.random.key(seed), 8)
    return {
        "q_raw": draw_q_raw(jax.random.fold_in(key_list[7], 71), 0),
        "k_raw": draw_k_raw(jax.random.fold_in(key_list[7], 71), 0),
        "values": bell_draw(key_list[2], (VIDEOS, SEQ_LEN, WIDTH), 1.0, 6.0, ((0, 4), (1, 128))),
        "d_attn": draw_d_attn(jax.random.fold_in(key_list[7], 71), 0),
        "q_gain": jnp.clip(1.0 + 0.1 * jax.random.normal(key_list[4], (WIDTH,), jnp.float32), 0.5, 1.5),
        "k_gain": jnp.clip(1.0 + 0.1 * jax.random.normal(key_list[5], (WIDTH,), jnp.float32), 0.5, 1.5),
        "kv_lists": draw_kv_lists(jax.random.fold_in(key_list[7], 71), 0),
    }


epsilon = 1e-06
top_precision = lax.Precision.HIGHEST

def half_round(values_in):
    return lax.optimization_barrier(values_in.astype(jnp.bfloat16)).astype(jnp.float32)

def norm_forward(raw_in, gain_vec):
    as_float = raw_in.astype(jnp.float32)
    inv_rms = lax.rsqrt(lax.optimization_barrier(jnp.mean(as_float * as_float, axis=-1, keepdims=True)) + epsilon)
    return (as_float, inv_rms, (as_float * inv_rms * gain_vec).astype(jnp.bfloat16))

def norm_backward(as_float, inv_rms, gain_vec, grad_norm):
    scaled = gain_vec * grad_norm
    inner_mean = lax.optimization_barrier(jnp.mean(scaled * as_float, axis=-1, keepdims=True))
    grad_raw = inv_rms * scaled - as_float * inv_rms * inv_rms * inv_rms * inner_mean
    gain_term = lax.optimization_barrier(jnp.sum(grad_norm * as_float * inv_rms, axis=tuple(range(grad_norm.ndim - 1))))
    return (grad_raw.astype(jnp.bfloat16), gain_term)

def one_video(q_raw, k_raw, values, d_attn, q_gain, k_gain, kv_lists):
    q_float, q_inv, q_norm = norm_forward(q_raw, q_gain)
    k_float, k_inv, k_norm = norm_forward(k_raw, k_gain)
    block_shape = (QBLOCKS, BLOCK, HEADS, HEAD_DIM)
    score_scale = 1.0 / math.sqrt(HEAD_DIM)
    queries = q_norm.reshape(block_shape).astype(jnp.float32)
    key_rows = k_norm.reshape(block_shape).astype(jnp.float32)
    value_rows = values.reshape(block_shape).astype(jnp.float32)
    grad_out = d_attn.reshape(block_shape).astype(jnp.float32)
    slot_count = kv_lists.shape[1]
    live_mask = kv_lists >= 0
    key_index = jnp.where(live_mask, kv_lists, 0).astype(jnp.int32)
    drop_index = jnp.where(live_mask, kv_lists, QBLOCKS).astype(jnp.int32)
    scores = []
    for slot_index in range(slot_count):
        picked = key_rows[key_index[:, slot_index]]
        raw_scores = jnp.einsum('bqhd,bkhd->bhqk', queries, picked, precision=top_precision) * score_scale
        scores.append(jnp.where(live_mask[:, slot_index][:, None, None, None], raw_scores, -jnp.inf))
    row_top = reduce(jnp.maximum, [lax.optimization_barrier(jnp.max(score_block, axis=-1)) for score_block in scores])
    row_total = reduce(jnp.add, [lax.optimization_barrier(jnp.sum(jnp.exp(score_block - row_top[..., None]), axis=-1)) for score_block in scores])
    log_total = row_top + jnp.log(row_total)
    halves = [half_round(jnp.exp(score_block - log_total[..., None])) for score_block in scores]
    attn_sum = jnp.zeros(block_shape, jnp.float32)
    for slot_index in range(slot_count):
        picked_values = value_rows[key_index[:, slot_index]]
        attn_sum = attn_sum + jnp.einsum('bhqk,bkhd->bqhd', halves[slot_index], picked_values, precision=top_precision)
    attn_out = attn_sum.astype(jnp.bfloat16).astype(jnp.float32)
    delta_rows = jnp.swapaxes(lax.optimization_barrier(jnp.sum(grad_out * attn_out, axis=-1)), 1, 2)
    grad_queries = jnp.zeros(block_shape, jnp.float32)
    grad_keys = jnp.zeros(block_shape, jnp.float32)
    grad_vals = jnp.zeros(block_shape, jnp.float32)
    for slot_index in range(slot_count):
        picked = key_rows[key_index[:, slot_index]]
        picked_values = value_rows[key_index[:, slot_index]]
        prob_full = jnp.exp(scores[slot_index] - log_total[..., None])
        grad_prob = jnp.einsum('bqhd,bkhd->bhqk', grad_out, picked_values, precision=top_precision)
        grad_score = half_round(prob_full * (grad_prob - delta_rows[..., None]))
        grad_queries = grad_queries + jnp.einsum('bhqk,bkhd->bqhd', grad_score, picked, precision=top_precision) * score_scale
        key_term = jnp.einsum('bhqk,bqhd->bkhd', grad_score, queries, precision=top_precision) * score_scale
        value_term = jnp.einsum('bhqk,bqhd->bkhd', halves[slot_index], grad_out, precision=top_precision)
        if slot_index > 0:
            key_term = half_round(key_term)
            value_term = half_round(value_term)
        grad_keys = grad_keys.at[drop_index[:, slot_index]].add(key_term, mode='drop')
        grad_vals = grad_vals.at[drop_index[:, slot_index]].add(value_term, mode='drop')
    flat_shape = (SEQ_LEN, WIDTH)
    d_q_raw, q_term = norm_backward(q_float, q_inv, q_gain, grad_queries.reshape(flat_shape))
    d_k_raw, k_term = norm_backward(k_float, k_inv, k_gain, grad_keys.reshape(flat_shape))
    d_values = grad_vals.reshape(flat_shape).astype(jnp.bfloat16)
    return (d_q_raw, d_k_raw, d_values, q_term, k_term)

def reference(q_raw, k_raw, values, d_attn, q_gain, k_gain, kv_lists):

    def per_video(video_items):
        return one_video(video_items[0], video_items[1], video_items[2], video_items[3], q_gain, k_gain, kv_lists)
    d_q_raw, d_k_raw, d_values, q_terms, k_terms = lax.map(per_video, (q_raw, k_raw, values, d_attn))
    norm_count = math.sqrt(VIDEOS * SEQ_LEN)
    return (d_q_raw, d_k_raw, d_values, lax.optimization_barrier(jnp.sum(q_terms, axis=0)) / norm_count, lax.optimization_barrier(jnp.sum(k_terms, axis=0)) / norm_count)
```

```python
import functools
import math

import jax
import jax.numpy as jnp
from jax import lax
from jax.experimental import pallas as pl
from jax.experimental.pallas import tpu as pltpu
from jax.sharding import PartitionSpec as P

HEADS = 20
HEAD_DIM = 128
BLOCK = 128
WIDTH = HEADS * HEAD_DIM
RING = 4
HOME = HEADS // RING
WINDOW = 5
CHAIN = RING + 4
ROWS = 16
SLOT_OF = (3, 1, 0, 2, 4)
EPSILON = 1e-06
SCALE = 1.0 / math.sqrt(HEAD_DIM)
MASKED = -1e30
MESH = pl.DeviceIdType.MESH


def kernel(
    sizes,
    q_ref, k_ref, v_ref, g_ref, q_gain_ref, k_gain_ref, kv_ref,
    dq_out, dk_out, dv_out, gain_out,
    raw, sent, inv, bias, kv, qg, acc, halo_out, halo_in, back, ret, fin,
    gain_own, gain_dp, gain_x, gain_z,
    load_sem, own_sem, fwd_send, fwd_recv, bias_send, bias_recv,
    halo_send, halo_recv, hg_send, hg_recv, ret_send, ret_recv, ret_own,
    gain_send, gain_recv, store_sem,
):
    n_x, n_z, n_dp = sizes
    n_seq = n_x * n_z * RING
    seq = lax.axis_index("seq")
    dp = lax.axis_index("dp")
    me = lax.rem(seq, RING)
    row = seq // RING
    x = lax.rem(row, n_x)
    z = row // n_x

    def ring(t):
        return (row * RING + t, dp)

    def side(s):
        step = n_seq - RING if s == 0 else RING
        return (lax.rem(seq + step, n_seq), dp)

    def at_x(t):
        return ((z * n_x + t) * RING + me, dp)

    def at_z(t):
        return ((t * n_x + x) * RING + me, dp)

    def ahead(d):
        return lax.rem(me + d, RING)

    def behind(d):
        return lax.rem(me + RING - d, RING)

    def head_cols(home, h):
        return pl.ds(pl.multiple_of((home * HOME + h) * HEAD_DIM, HEAD_DIM), HEAD_DIM)

    def chain_rows(block, count=1):
        return pl.ds(pl.multiple_of((block + 2) * BLOCK, BLOCK), count * BLOCK)

    loads = [
        pltpu.make_async_copy(k_ref, raw.at[0], load_sem.at[0]),
        pltpu.make_async_copy(q_ref, raw.at[1], load_sem.at[1]),
        pltpu.make_async_copy(v_ref, sent.at[1], load_sem.at[2]),
        pltpu.make_async_copy(g_ref, sent.at[3], load_sem.at[3]),
    ]
    for load in loads:
        load.start()

    partners = [ring(ahead(d)) for d in range(1, RING)] + [side(0), side(1)]
    partners += [(seq, lax.rem(dp + d, n_dp)) for d in range(1, n_dp)]
    partners += [at_x(lax.rem(x + d, n_x)) for d in range(1, n_x)]
    partners += [at_z(lax.rem(z + d, n_z)) for d in range(1, n_z)]
    barrier = pltpu.get_barrier_semaphore()
    for partner in partners:
        pl.semaphore_signal(barrier, 1, device_id=partner, device_id_type=MESH)

    def normed(which, gain_ref):
        def step(i, carry):
            rows = pl.ds(pl.multiple_of(i * ROWS, ROWS), ROWS)
            value = raw[which, rows, :].astype(jnp.float32)
            mean = jnp.sum(value * value, axis=-1, keepdims=True) * (1.0 / WIDTH)
            scale = lax.rsqrt(mean + EPSILON)
            inv[which, rows, :] = jnp.broadcast_to(scale, (ROWS, HEAD_DIM))
            sent[2 * which, rows, :] = (value * scale * gain_ref[...]).astype(jnp.bfloat16)
            return carry

        lax.fori_loop(0, BLOCK // ROWS, step, 0)

    bias[me] = jnp.zeros((8, HEAD_DIM), jnp.float32)
    for w in range(WINDOW):
        level = jnp.where(kv_ref[0, SLOT_OF[w]] >= 0, 0.0, MASKED).astype(jnp.float32)
        bias[me, w : w + 1, :] = jnp.full((1, HEAD_DIM), level, jnp.float32)

    def bias_copy(d):
        return pltpu.make_async_remote_copy(
            bias.at[me], bias.at[me], bias_send.at[d - 1], bias_recv.at[d - 1],
            device_id=ring(ahead(d)), device_id_type=MESH,
        )

    def bias_arrival(d):
        return pltpu.make_async_remote_copy(
            bias.at[behind(d)], bias.at[behind(d)], bias_send.at[d - 1], bias_recv.at[d - 1],
            device_id=ring(ahead(d)), device_id_type=MESH,
        )

    def forward(h, d, g):
        home = ahead(d)
        source = sent.at[pl.ds(2 * g, 2), :, head_cols(home, h)]
        target = kv.at[h, :, chain_rows(me), :] if g == 0 else qg.at[h, me]
        return pltpu.make_async_remote_copy(
            source, target, fwd_send.at[h, d - 1, g], fwd_recv.at[h, d - 1, g],
            device_id=ring(home), device_id_type=MESH,
        )

    def arrival(h, d, g):
        home = behind(d)
        target = kv.at[h, :, chain_rows(home), :] if g == 0 else qg.at[h, home]
        return pltpu.make_async_remote_copy(
            target, target, fwd_send.at[h, d - 1, g], fwd_recv.at[h, d - 1, g],
            device_id=ring(ahead(d)), device_id_type=MESH,
        )

    def own(h, g):
        source = sent.at[pl.ds(2 * g, 2), :, head_cols(me, h)]
        target = kv.at[h, :, chain_rows(me), :] if g == 0 else qg.at[h, me]
        return pltpu.make_async_copy(source, target, own_sem.at[h, g])

    def halo(h, s):
        mine = pl.ds((2 if s == 0 else RING) * BLOCK, 2 * BLOCK)
        theirs = pl.ds((RING + 2 if s == 0 else 0) * BLOCK, 2 * BLOCK)
        return pltpu.make_async_remote_copy(
            kv.at[h, :, mine, :], kv.at[h, :, theirs, :], halo_send.at[h, s], halo_recv.at[h, s],
            device_id=side(s), device_id_type=MESH,
        )

    def halo_back(h, s):
        return pltpu.make_async_remote_copy(
            halo_out.at[h, s], halo_in.at[h, 1 - s], hg_send.at[h, s], hg_recv.at[h, s],
            device_id=side(s), device_id_type=MESH,
        )

    def give_back(h, d):
        home = ahead(d)
        return pltpu.make_async_remote_copy(
            back.at[h, home], ret.at[:, :, head_cols(me, h)], ret_send.at[h, d - 1], ret_recv.at[h, d - 1],
            device_id=ring(home), device_id_type=MESH,
        )

    def given(h, d):
        target = ret.at[:, :, head_cols(behind(d), h)]
        return pltpu.make_async_remote_copy(
            target, target, ret_send.at[h, d - 1], ret_recv.at[h, d - 1],
            device_id=ring(ahead(d)), device_id_type=MESH,
        )

    def keep_back(h):
        return pltpu.make_async_copy(back.at[h, me], ret.at[:, :, head_cols(me, h)], ret_own.at[h])

    loads[0].wait()
    normed(0, k_gain_ref)
    loads[1].wait()
    normed(1, q_gain_ref)
    loads[2].wait()
    loads[3].wait()
    pl.semaphore_wait(barrier, len(partners))

    for d in range(1, RING):
        bias_copy(d).start()

    def send_head(h, carry):
        for g in range(2):
            for d in (2, 1, 3):
                forward(h, d, g).start()
            own(h, g).start()
        return carry

    lax.fori_loop(0, HOME, send_head, 0)
    for d in range(1, RING):
        bias_arrival(d).wait_recv()

    factor = SCALE * math.log2(math.e)
    by_row = (((1,), (1,)), ((), ()))
    by_col = (((0,), (0,)), ((), ()))

    def return_head(h):
        for d in (2, 1, 3):
            give_back(h, d).start()
        keep_back(h).start()

    def work(h, hold):
        for g in range(2):
            own(h, g).wait()
            for d in range(1, RING):
                arrival(h, d, g).wait_recv()
            if g == 0:
                for s in range(2):
                    halo(h, s).start()
        hold()
        acc[...] = jnp.zeros_like(acc)
        for s in range(2):
            halo(h, s).wait_recv()
        gain_q = jnp.zeros((1, HEAD_DIM), jnp.float32)
        for b in range(RING):
            span = slice(b * BLOCK, (b + WINDOW) * BLOCK)
            keys = kv[h, 0, span, :]
            vals = kv[h, 1, span, :]
            query = qg[h, b, 0]
            grad = qg[h, b, 1]
            level = bias[b][:WINDOW].reshape(WINDOW, 1, HEAD_DIM)
            score = lax.dot_general(keys, query, by_row, preferred_element_type=jnp.float32)
            score = score.reshape(WINDOW, BLOCK, HEAD_DIM) * factor + level
            score = score.reshape(WINDOW * BLOCK, HEAD_DIM)
            top = jnp.max(score, axis=0, keepdims=True)
            weight = jnp.exp2(score - top)
            prob = weight * (1.0 / jnp.sum(weight, axis=0, keepdims=True))
            d_prob = lax.dot_general(vals, grad, by_row, preferred_element_type=jnp.float32)
            delta = jnp.sum(prob * d_prob, axis=0, keepdims=True)
            d_score = (prob * (d_prob - delta)).astype(jnp.bfloat16)
            acc[0, span, :] += jnp.dot(d_score, query, preferred_element_type=jnp.float32)
            acc[1, span, :] += jnp.dot(
                prob.astype(jnp.bfloat16), grad, preferred_element_type=jnp.float32
            )
            d_query = lax.dot_general(d_score, keys, by_col, preferred_element_type=jnp.float32) * SCALE
            back[h, b, 0] = d_query.astype(jnp.bfloat16)
            gain_q += jnp.sum(d_query * query.astype(jnp.float32), axis=0, keepdims=True)
        gain_k = jnp.zeros((1, HEAD_DIM), jnp.float32)
        for c in range(CHAIN):
            part = slice(c * BLOCK, (c + 1) * BLOCK)
            gain_k += jnp.sum(acc[0, part, :] * kv[h, 0, part, :].astype(jnp.float32), axis=0, keepdims=True)
        for s in range(2):
            part = slice(0, 2 * BLOCK) if s == 0 else slice((RING + 2) * BLOCK, CHAIN * BLOCK)
            halo_out[h, s, 0] = (acc[0, part, :] * SCALE).astype(jnp.bfloat16)
            halo_out[h, s, 1] = acc[1, part, :].astype(jnp.bfloat16)
            halo_back(h, s).start()
        gain_own[pl.ds(h, 1), :] = gain_q / q_gain_ref[:, head_cols(me, h)]
        gain_own[pl.ds(h + 8, 1), :] = gain_k * SCALE / k_gain_ref[:, head_cols(me, h)]

    def settle(h):
        for s in range(2):
            halo_back(h, s).wait_recv()
        for b in range(RING):
            part = slice((b + 2) * BLOCK, (b + 3) * BLOCK)
            came = slice((b % 2) * BLOCK, (b % 2 + 1) * BLOCK)
            for t in range(2):
                extra = halo_in[h, b // 2, t, came, :].astype(jnp.float32)
                own_part = acc[t, part, :]
                if t == 0:
                    own_part = own_part * SCALE
                back[h, b, t + 1] = (own_part + extra).astype(jnp.bfloat16)

    gain_own[...] = jnp.zeros_like(gain_own)

    def early(h, carry):
        work(h, lambda: None)
        settle(h)
        return carry

    lax.fori_loop(0, HOME - 1, early, 0)

    def release():
        def step(h, carry):
            return_head(h)
            return carry

        lax.fori_loop(0, HOME - 1, step, 0)

    last = HOME - 1
    work(last, release)

    gain_stages = (
        (gain_dp, dp, n_dp, lambda t: (seq, t), 0),
        (gain_x, x, n_x, at_x, n_dp),
        (gain_z, z, n_z, at_z, n_dp + n_x),
        (fin, me, RING, ring, n_dp + n_x + n_z),
    )

    def gain_copy(stage, d, mine):
        slots, place, count, device, base = gain_stages[stage]
        slot = slots.at[place if mine else lax.rem(place + count - d, count)]
        return pltpu.make_async_remote_copy(
            slot, slot, gain_send.at[base + d], gain_recv.at[base + d],
            device_id=device(lax.rem(place + d, count)), device_id_type=MESH,
        )

    def gain_start(stage, value):
        slots, place, count = gain_stages[stage][:3]
        slots[place] = value
        for d in range(1, count):
            gain_copy(stage, d, True).start()

    def gain_finish(stage):
        slots, count = gain_stages[stage][0], gain_stages[stage][2]
        for d in range(1, count):
            gain_copy(stage, d, False).wait_recv()
        total = slots[0]
        for t in range(1, count):
            total = total + slots[t]
        return total

    gain_start(0, gain_own[...])
    settle(last)
    return_head(last)
    gain_start(1, gain_finish(0))
    gain_start(2, gain_finish(1))
    n_tokens = n_seq * BLOCK * n_dp
    gain_start(3, gain_finish(2) * (1.0 / math.sqrt(n_tokens)))

    def await_head(h, carry):
        for d in range(1, RING):
            given(h, d).wait_recv()
        keep_back(h).wait()
        return carry

    lax.fori_loop(0, HOME, await_head, 0)
    values_out = pltpu.make_async_copy(ret.at[2], dv_out, store_sem)
    values_out.start()

    def finish(which, gain_ref, out_ref):
        def step(i, carry):
            rows = pl.ds(pl.multiple_of(i * ROWS, ROWS), ROWS)
            value = raw[1 - which, rows, :].astype(jnp.float32)
            scaled = gain_ref[...] * ret[which, rows, :].astype(jnp.float32)
            mean = jnp.sum(scaled * value, axis=-1, keepdims=True) * (1.0 / WIDTH)
            scale = inv[1 - which, rows, :][:, :1]
            out_ref[rows, :] = (scale * scaled - value * (scale * scale * scale * mean)).astype(jnp.bfloat16)
            return carry

        lax.fori_loop(0, BLOCK // ROWS, step, 0)

    finish(0, q_gain_ref, dq_out)
    finish(1, k_gain_ref, dk_out)
    gain_finish(3)
    for t in range(RING):
        gain_out[t] = fin[t]
    values_out.wait()

    for d in range(1, RING):
        bias_copy(d).wait_send()

    def drain(h, carry):
        for d in range(1, RING):
            for g in range(2):
                forward(h, d, g).wait_send()
            give_back(h, d).wait_send()
        for s in range(2):
            halo(h, s).wait_send()
            halo_back(h, s).wait_send()
        return carry

    lax.fori_loop(0, HOME, drain, 0)
    for stage in range(4):
        for d in range(1, gain_stages[stage][2]):
            gain_copy(stage, d, True).wait_send()


def body(sizes, q_raw, k_raw, values, d_attn, q_gain, k_gain, kv_lists):
    n_x, n_z, n_dp = sizes
    flat = (BLOCK, WIDTH)
    half = jnp.bfloat16
    anywhere = pl.BlockSpec(memory_space=pl.ANY)
    vmem = pl.BlockSpec(memory_space=pltpu.VMEM)
    dma = pltpu.SemaphoreType.DMA
    n_gain = n_dp + n_x + n_z + RING
    pair = (2, 2 * BLOCK, HEAD_DIM)
    d_q, d_k, d_v, gains = pl.pallas_call(
        functools.partial(kernel, sizes),
        out_shape=(
            jax.ShapeDtypeStruct(flat, half),
            jax.ShapeDtypeStruct(flat, half),
            jax.ShapeDtypeStruct(flat, half),
            jax.ShapeDtypeStruct((RING, 16, HEAD_DIM), jnp.float32),
        ),
        in_specs=[anywhere] * 4 + [vmem, vmem, pl.BlockSpec(memory_space=pltpu.SMEM)],
        out_specs=(vmem, vmem, anywhere, vmem),
        scratch_shapes=[
            pltpu.VMEM((2,) + flat, half),
            pltpu.VMEM((4,) + flat, half),
            pltpu.VMEM((2, BLOCK, HEAD_DIM), jnp.float32),
            pltpu.VMEM((RING, 8, HEAD_DIM), jnp.float32),
            pltpu.VMEM((HOME, 2, CHAIN * BLOCK, HEAD_DIM), half),
            pltpu.VMEM((HOME, RING, 2, BLOCK, HEAD_DIM), half),
            pltpu.VMEM((2, CHAIN * BLOCK, HEAD_DIM), jnp.float32),
            pltpu.VMEM((HOME, 2) + pair, half),
            pltpu.VMEM((HOME, 2) + pair, half),
            pltpu.VMEM((HOME, RING, 3, BLOCK, HEAD_DIM), half),
            pltpu.VMEM((3,) + flat, half),
            pltpu.VMEM((RING, 16, HEAD_DIM), jnp.float32),
            pltpu.VMEM((16, HEAD_DIM), jnp.float32),
            pltpu.VMEM((n_dp, 16, HEAD_DIM), jnp.float32),
            pltpu.VMEM((n_x, 16, HEAD_DIM), jnp.float32),
            pltpu.VMEM((n_z, 16, HEAD_DIM), jnp.float32),
            dma((4,)),
            dma((HOME, 2)),
            dma((HOME, RING - 1, 2)),
            dma((HOME, RING - 1, 2)),
            dma((RING - 1,)),
            dma((RING - 1,)),
            dma((HOME, 2)),
            dma((HOME, 2)),
            dma((HOME, 2)),
            dma((HOME, 2)),
            dma((HOME, RING - 1)),
            dma((HOME, RING - 1)),
            dma((HOME,)),
            dma((n_gain,)),
            dma((n_gain,)),
            dma,
        ],
        compiler_params=pltpu.CompilerParams(
            collective_id=0, has_side_effects=True, vmem_limit_bytes=40 * 1024 * 1024
        ),
    )(
        q_raw.reshape(flat), k_raw.reshape(flat), values.reshape(flat), d_attn.reshape(flat),
        q_gain.reshape(1, WIDTH), k_gain.reshape(1, WIDTH), kv_lists,
    )
    shape = q_raw.shape
    q_sum = gains[:, :HOME].reshape(WIDTH)
    k_sum = gains[:, 8 : 8 + HOME].reshape(WIDTH)
    return d_q.reshape(shape), d_k.reshape(shape), d_v.reshape(shape), q_sum, k_sum


def solution(mesh):
    rows = mesh.shape["seq"] // RING
    n_x = 4 if rows % 4 == 0 and rows > 4 else 2
    sizes = (n_x, rows // n_x, mesh.shape["dp"])
    split = P("dp", "seq", None)
    return jax.shard_map(
        functools.partial(body, sizes),
        mesh=mesh,
        in_specs=(split, split, split, split, P(), P(), P("seq", None)),
        out_specs=(split, split, split, P(), P()),
        check_vma=False,
    )
```

```python
import functools
import math

import jax
import jax.numpy as jnp
from jax import lax
from jax.experimental import pallas as pl
from jax.experimental.pallas import tpu as pltpu
from jax.sharding import PartitionSpec as P

HEADS = 20
HEAD_DIM = 128
BLOCK = 128
WIDTH = HEADS * HEAD_DIM
RING = 4
HOME = HEADS // RING
WINDOW = 5
CHAIN = RING + 4
ROWS = 16
SLOT_OF = (3, 1, 0, 2, 4)
EPSILON = 1e-06
SCALE = 1.0 / math.sqrt(HEAD_DIM)
MASKED = -1e30
MESH = pl.DeviceIdType.MESH


def kernel(
    sizes,
    q_ref, k_ref, v_ref, g_ref, q_gain_ref, k_gain_ref, kv_ref,
    dq_out, dk_out, dv_out, gain_out,
    raw, sent, inv, gains, bias_own, bias, chain, acc, halo_out, halo_in, back, ret, fin,
    gain_own, gain_dp, gain_x, gain_z,
    load_sem, fwd_send, fwd_recv, bias_send, bias_recv,
    halo_send, halo_recv, hg_send, hg_recv, ret_send, ret_recv,
    gain_send, gain_recv, store_sem,
):
    n_x, n_z, n_dp = sizes
    n_seq = n_x * n_z * RING
    seq = lax.axis_index("seq")
    dp = lax.axis_index("dp")
    me = lax.rem(seq, RING)
    row = seq // RING
    x = lax.rem(row, n_x)
    z = row // n_x

    across = lax.rem(dp + n_dp // 2, n_dp)

    def ring(t):
        return (row * RING + t, dp)

    def over(t):
        return (row * RING + t, across)

    def side(s):
        step = n_seq - RING if s == 0 else RING
        return (lax.rem(seq + step, n_seq), dp)

    def at_x(t):
        return ((z * n_x + t) * RING + me, dp)

    def at_z(t):
        return ((t * n_x + x) * RING + me, dp)

    def ahead(d):
        return lax.rem(me + d, RING)

    def behind(d):
        return lax.rem(me + RING - d, RING)

    def head_cols(home, h):
        return pl.ds(pl.multiple_of((home * HOME + h) * HEAD_DIM, HEAD_DIM), HEAD_DIM)

    def chain_rows(block, count=1):
        return pl.ds(pl.multiple_of((block + 2) * BLOCK, BLOCK), count * BLOCK)

    loads = [
        pltpu.make_async_copy(k_ref, raw.at[0], load_sem.at[0]),
        pltpu.make_async_copy(q_ref, raw.at[1], load_sem.at[1]),
        pltpu.make_async_copy(g_ref, sent.at[0], load_sem.at[2]),
        pltpu.make_async_copy(v_ref, sent.at[1], load_sem.at[3]),
    ]
    for load in loads:
        load.start()

    partners = [over(t) for t in range(RING)] + [side(0), side(1)]
    partners += [ring(ahead(d)) for d in range(1, RING)]
    partners += [(seq, lax.rem(dp + d, n_dp)) for d in range(1, n_dp)]
    partners += [at_x(lax.rem(x + d, n_x)) for d in range(1, n_x)]
    partners += [at_z(lax.rem(z + d, n_z)) for d in range(1, n_z)]
    barrier = pltpu.get_barrier_semaphore()
    for partner in partners:
        pl.semaphore_signal(barrier, 1, device_id=partner, device_id_type=MESH)

    gains[0] = k_gain_ref[...].reshape(1, WIDTH)
    gains[1] = q_gain_ref[...].reshape(1, WIDTH)

    def normed(which):
        def step(i, carry):
            rows = pl.ds(pl.multiple_of(i * ROWS, ROWS), ROWS)
            value = raw[which, rows, :].astype(jnp.float32)
            mean = jnp.sum(value * value, axis=-1, keepdims=True) * (1.0 / WIDTH)
            scale = lax.rsqrt(mean + EPSILON)
            inv[which, rows, :] = jnp.broadcast_to(scale, (ROWS, HEAD_DIM))
            sent[2 + which, rows, :] = (value * scale * gains[which]).astype(jnp.bfloat16)
            return carry

        lax.fori_loop(0, BLOCK // ROWS, step, 0)

    bias_own[...] = jnp.zeros((8, HEAD_DIM), jnp.float32)
    for w in range(WINDOW):
        level = jnp.where(kv_ref[0, SLOT_OF[w]] >= 0, 0.0, MASKED).astype(jnp.float32)
        bias_own[w : w + 1, :] = jnp.full((1, HEAD_DIM), level, jnp.float32)

    def bias_copy(d):
        return pltpu.make_async_remote_copy(
            bias_own, bias.at[me], bias_send.at[d], bias_recv.at[d],
            device_id=over(ahead(d)), device_id_type=MESH,
        )

    def bias_arrival(d):
        return pltpu.make_async_remote_copy(
            bias_own, bias.at[behind(d)], bias_send.at[d], bias_recv.at[d],
            device_id=over(ahead(d)), device_id_type=MESH,
        )

    def forward(h, d, g):
        home = ahead(d)
        part = pl.ds(2 * g, 2)
        return pltpu.make_async_remote_copy(
            sent.at[part, :, head_cols(home, h)], chain.at[h, part, chain_rows(me), :],
            fwd_send.at[h, d, g], fwd_recv.at[h, d, g],
            device_id=over(home), device_id_type=MESH,
        )

    def arrival(h, d, g):
        target = chain.at[h, pl.ds(2 * g, 2), chain_rows(behind(d)), :]
        return pltpu.make_async_remote_copy(
            target, target, fwd_send.at[h, d, g], fwd_recv.at[h, d, g],
            device_id=over(ahead(d)), device_id_type=MESH,
        )

    def halo(h, s):
        mine = pl.ds((2 if s == 0 else RING) * BLOCK, 2 * BLOCK)
        theirs = pl.ds((RING + 2 if s == 0 else 0) * BLOCK, 2 * BLOCK)
        return pltpu.make_async_remote_copy(
            chain.at[h, 1:3, mine, :], chain.at[h, 1:3, theirs, :], halo_send.at[h, s], halo_recv.at[h, s],
            device_id=side(s), device_id_type=MESH,
        )

    def halo_back(h, s):
        return pltpu.make_async_remote_copy(
            halo_out.at[h, s], halo_in.at[h, 1 - s], hg_send.at[h, s], hg_recv.at[h, s],
            device_id=side(s), device_id_type=MESH,
        )

    def target_of(t, home, h):
        cols = head_cols(home, h)
        return ret.at[:, :, cols] if t == 0 else dv_out.at[:, cols]

    def give_back(h, d, t):
        home = ahead(d)
        return pltpu.make_async_remote_copy(
            back.at[h, home, 0:2] if t == 0 else back.at[h, home, 2], target_of(t, me, h),
            ret_send.at[h, d, t], ret_recv.at[h, d, t],
            device_id=over(home), device_id_type=MESH,
        )

    def given(h, d, t):
        target = target_of(t, behind(d), h)
        return pltpu.make_async_remote_copy(
            target, target, ret_send.at[h, d, t], ret_recv.at[h, d, t],
            device_id=over(ahead(d)), device_id_type=MESH,
        )

    loads[0].wait()
    normed(0)
    loads[1].wait()
    normed(1)
    loads[2].wait()
    loads[3].wait()
    pl.semaphore_wait(barrier, len(partners))

    def send_head(h, carry):
        for g in range(2):
            for d in range(RING):
                forward(h, d, g).start()
        return carry

    send_head(0, 0)
    for d in range(RING):
        bias_copy(d).start()
    send_head(1, 0)

    factor = SCALE * math.log2(math.e)
    by_row = (((1,), (1,)), ((), ()))
    by_col = (((0,), (0,)), ((), ()))

    def return_head(h, t):
        for d in range(RING):
            give_back(h, d, t).start()

    def receive(h):
        for g in range(2):
            for d in range(RING):
                arrival(h, d, g).wait_recv()
        for s in range(2):
            halo(h, s).start()

    def work(h):
        acc[...] = jnp.zeros_like(acc)
        for s in range(2):
            halo(h, s).wait_recv()
        gain_q = jnp.zeros((1, HEAD_DIM), jnp.float32)
        for b in range(RING):
            span = slice(b * BLOCK, (b + WINDOW) * BLOCK)
            mine = slice((b + 2) * BLOCK, (b + 3) * BLOCK)
            vals = chain[h, 1, span, :]
            keys = chain[h, 2, span, :]
            grad = chain[h, 0, mine, :]
            query = chain[h, 3, mine, :]
            level = bias[b][:WINDOW].reshape(WINDOW, 1, HEAD_DIM)
            score = lax.dot_general(keys, query, by_row, preferred_element_type=jnp.float32)
            score = score.reshape(WINDOW, BLOCK, HEAD_DIM) * factor + level
            score = score.reshape(WINDOW * BLOCK, HEAD_DIM)
            top = jnp.max(score, axis=0, keepdims=True)
            weight = jnp.exp2(score - top)
            prob = weight * (1.0 / jnp.sum(weight, axis=0, keepdims=True))
            d_prob = lax.dot_general(vals, grad, by_row, preferred_element_type=jnp.float32)
            delta = jnp.sum(prob * d_prob, axis=0, keepdims=True)
            d_score = (prob * (d_prob - delta)).astype(jnp.bfloat16)
            acc[0, span, :] += jnp.dot(d_score, query, preferred_element_type=jnp.float32)
            acc[1, span, :] += jnp.dot(
                prob.astype(jnp.bfloat16), grad, preferred_element_type=jnp.float32
            )
            d_query = lax.dot_general(d_score, keys, by_col, preferred_element_type=jnp.float32) * SCALE
            back[h, b, 0] = d_query.astype(jnp.bfloat16)
            gain_q += jnp.sum(d_query * query.astype(jnp.float32), axis=0, keepdims=True)
        gain_k = jnp.zeros((1, HEAD_DIM), jnp.float32)
        for c in range(CHAIN):
            part = slice(c * BLOCK, (c + 1) * BLOCK)
            gain_k += jnp.sum(acc[0, part, :] * chain[h, 2, part, :].astype(jnp.float32), axis=0, keepdims=True)
        for s in range(2):
            part = slice(0, 2 * BLOCK) if s == 0 else slice((RING + 2) * BLOCK, CHAIN * BLOCK)
            halo_out[h, s, 0] = (acc[0, part, :] * SCALE).astype(jnp.bfloat16)
            halo_out[h, s, 1] = acc[1, part, :].astype(jnp.bfloat16)
            halo_back(h, s).start()
        gain_own[pl.ds(h, 1), :] = gain_q / gains[1, :, head_cols(me, h)]
        gain_own[pl.ds(h + 8, 1), :] = gain_k * SCALE / gains[0, :, head_cols(me, h)]

    def settle(h):
        for s in range(2):
            halo_back(h, s).wait_recv()
        for b in range(RING):
            part = slice((b + 2) * BLOCK, (b + 3) * BLOCK)
            came = slice((b % 2) * BLOCK, (b % 2 + 1) * BLOCK)
            for t in range(2):
                extra = halo_in[h, b // 2, t, came, :].astype(jnp.float32)
                own_part = acc[t, part, :]
                if t == 0:
                    own_part = own_part * SCALE
                back[h, b, t + 1] = (own_part + extra).astype(jnp.bfloat16)

    gain_own[...] = jnp.zeros_like(gain_own)

    last = HOME - 1
    receive(0)
    send_head(2, 0)
    for d in range(RING):
        bias_arrival(d).wait_recv()
    work(0)

    def middle(h, carry):
        receive(h)

        @pl.when(h + 2 < HOME)
        def _():
            send_head(h + 2, 0)

        settle(h - 1)
        return_head(h - 1, 0)
        work(h)
        return carry

    lax.fori_loop(1, last, middle, 0)
    receive(last)
    settle(last - 1)
    return_head(last - 1, 0)
    work(last)

    gain_stages = (
        (gain_dp, dp, n_dp, lambda t: (seq, t), 0),
        (gain_x, x, n_x, at_x, n_dp),
        (gain_z, z, n_z, at_z, n_dp + n_x),
        (fin, me, RING, ring, n_dp + n_x + n_z),
    )

    def gain_copy(stage, d, mine):
        slots, place, count, device, base = gain_stages[stage]
        slot = slots.at[place if mine else lax.rem(place + count - d, count)]
        return pltpu.make_async_remote_copy(
            slot, slot, gain_send.at[base + d], gain_recv.at[base + d],
            device_id=device(lax.rem(place + d, count)), device_id_type=MESH,
        )

    def gain_start(stage, value):
        slots, place, count = gain_stages[stage][:3]
        slots[place] = value
        for d in range(1, count):
            gain_copy(stage, d, True).start()

    def gain_finish(stage):
        slots, count = gain_stages[stage][0], gain_stages[stage][2]
        for d in range(1, count):
            gain_copy(stage, d, False).wait_recv()
        total = slots[0]
        for t in range(1, count):
            total = total + slots[t]
        return total

    gain_start(0, gain_own[...])
    settle(last)
    return_head(last, 0)
    for h in range(HOME):
        return_head(h, 1)
    gain_start(1, gain_finish(0))
    gain_start(2, gain_finish(1))
    n_tokens = n_seq * BLOCK * n_dp
    gain_start(3, gain_finish(2) * (1.0 / math.sqrt(n_tokens)))

    def await_returns(t):
        def step(h, carry):
            for d in range(RING):
                given(h, d, t).wait_recv()
            return carry

        lax.fori_loop(0, HOME, step, 0)

    await_returns(0)

    def finish(which, out_ref):
        def step(i, carry):
            rows = pl.ds(pl.multiple_of(i * ROWS, ROWS), ROWS)
            value = raw[1 - which, rows, :].astype(jnp.float32)
            scaled = gains[1 - which] * ret[which, rows, :].astype(jnp.float32)
            mean = jnp.sum(scaled * value, axis=-1, keepdims=True) * (1.0 / WIDTH)
            scale = inv[1 - which, rows, :][:, :1]
            ret[which, rows, :] = (scale * scaled - value * (scale * scale * scale * mean)).astype(jnp.bfloat16)
            return carry

        lax.fori_loop(0, BLOCK // ROWS, step, 0)
        store = pltpu.make_async_copy(ret.at[which], out_ref, store_sem.at[which])
        store.start()
        return store

    stores = [finish(0, dq_out), finish(1, dk_out)]
    gain_finish(3)
    for t in range(RING):
        gain_out[t] = fin[t]
    await_returns(1)
    for store in stores:
        store.wait()

    for d in range(RING):
        bias_copy(d).wait_send()

    def drain(h, carry):
        for d in range(RING):
            for g in range(2):
                forward(h, d, g).wait_send()
                give_back(h, d, g).wait_send()
        for s in range(2):
            halo(h, s).wait_send()
            halo_back(h, s).wait_send()
        return carry

    lax.fori_loop(0, HOME, drain, 0)
    for stage in range(4):
        for d in range(1, gain_stages[stage][2]):
            gain_copy(stage, d, True).wait_send()


def hand_over(dq_ref, dk_ref, dv_ref, gain_ref, dq_out, dk_out, dv_out, q_sum, k_sum, held, in_sem, out_sem):
    loads = [
        pltpu.make_async_copy(src, held.at[i], in_sem.at[i]) for i, src in enumerate((dq_ref, dk_ref, dv_ref))
    ]
    stores = [
        pltpu.make_async_copy(held.at[i], dst, out_sem.at[i]) for i, dst in enumerate((dq_out, dk_out, dv_out))
    ]
    for load in loads:
        load.start()
    for load, store in zip(loads, stores):
        load.wait()
        store.start()
    for home in range(RING):
        for h in range(HOME):
            cols = pl.ds((home * HOME + h) * HEAD_DIM, HEAD_DIM)
            q_sum[cols] = gain_ref[home, h]
            k_sum[cols] = gain_ref[home, 8 + h]
    for store in stores:
        store.wait()


def body(sizes, q_raw, k_raw, values, d_attn, q_gain, k_gain, kv_lists):
    n_x, n_z, n_dp = sizes
    flat = (BLOCK, WIDTH)
    half = jnp.bfloat16
    anywhere = pl.BlockSpec(memory_space=pl.ANY)
    vmem = pl.BlockSpec(memory_space=pltpu.VMEM)
    dma = pltpu.SemaphoreType.DMA
    n_gain = n_dp + n_x + n_z + RING
    pair = (2, 2 * BLOCK, HEAD_DIM)
    d_q, d_k, d_v, gains = pl.pallas_call(
        functools.partial(kernel, sizes),
        out_shape=(
            jax.ShapeDtypeStruct(flat, half),
            jax.ShapeDtypeStruct(flat, half),
            jax.ShapeDtypeStruct(flat, half),
            jax.ShapeDtypeStruct((RING, 16, HEAD_DIM), jnp.float32),
        ),
        in_specs=[anywhere] * 4 + [vmem, vmem, pl.BlockSpec(memory_space=pltpu.SMEM)],
        out_specs=(anywhere, anywhere, anywhere, vmem),
        scratch_shapes=[
            pltpu.VMEM((2,) + flat, half),
            pltpu.VMEM((4,) + flat, half),
            pltpu.VMEM((2, BLOCK, HEAD_DIM), jnp.float32),
            pltpu.VMEM((2, 1, WIDTH), jnp.float32),
            pltpu.VMEM((8, HEAD_DIM), jnp.float32),
            pltpu.VMEM((RING, 8, HEAD_DIM), jnp.float32),
            pltpu.VMEM((HOME, 4, CHAIN * BLOCK, HEAD_DIM), half),
            pltpu.VMEM((2, CHAIN * BLOCK, HEAD_DIM), jnp.float32),
            pltpu.VMEM((HOME, 2) + pair, half),
            pltpu.VMEM((HOME, 2) + pair, half),
            pltpu.VMEM((HOME, RING, 3, BLOCK, HEAD_DIM), half),
            pltpu.VMEM((2,) + flat, half),
            pltpu.VMEM((RING, 16, HEAD_DIM), jnp.float32),
            pltpu.VMEM((16, HEAD_DIM), jnp.float32),
            pltpu.VMEM((n_dp, 16, HEAD_DIM), jnp.float32),
            pltpu.VMEM((n_x, 16, HEAD_DIM), jnp.float32),
            pltpu.VMEM((n_z, 16, HEAD_DIM), jnp.float32),
            dma((4,)),
            dma((HOME, RING, 2)),
            dma((HOME, RING, 2)),
            dma((RING,)),
            dma((RING,)),
            dma((HOME, 2)),
            dma((HOME, 2)),
            dma((HOME, 2)),
            dma((HOME, 2)),
            dma((HOME, RING, 2)),
            dma((HOME, RING, 2)),
            dma((n_gain,)),
            dma((n_gain,)),
            dma((2,)),
        ],
        compiler_params=pltpu.CompilerParams(
            collective_id=0, has_side_effects=True, vmem_limit_bytes=62 * 1024 * 1024
        ),
    )(
        q_raw.reshape(flat), k_raw.reshape(flat), values.reshape(flat), d_attn.reshape(flat),
        q_gain, k_gain, kv_lists,
    )
    out = pl.pallas_call(
        hand_over,
        out_shape=(jax.ShapeDtypeStruct(flat, half),) * 3 + (jax.ShapeDtypeStruct((WIDTH,), jnp.float32),) * 2,
        in_specs=[anywhere] * 3 + [vmem],
        out_specs=(anywhere,) * 3 + (vmem,) * 2,
        scratch_shapes=[pltpu.VMEM((3,) + flat, half), dma((3,)), dma((3,))],
    )(d_q, d_k, d_v, gains)
    shape = q_raw.shape
    return tuple(part.reshape(shape) for part in out[:3]) + out[3:]


def solution(mesh):
    rows = mesh.shape["seq"] // RING
    n_x = 4 if rows % 4 == 0 and rows > 4 else 2
    sizes = (n_x, rows // n_x, mesh.shape["dp"])
    split = P("dp", "seq", None)
    return jax.shard_map(
        functools.partial(body, sizes),
        mesh=mesh,
        in_specs=(split, split, split, split, P(), P(), P("seq", None)),
        out_specs=(split, split, split, P(), P()),
        check_vma=False,
    )
```

```python
import functools
import math

import jax
import jax.numpy as jnp
from jax import lax
from jax.experimental import pallas as pl
from jax.experimental.pallas import tpu as pltpu
from jax.sharding import PartitionSpec as P

HEADS = 20
HEAD_DIM = 128
BLOCK = 128
WIDTH = HEADS * HEAD_DIM
RING = 4
HOME = HEADS // RING
WINDOW = 5
CHAIN = RING + 4
ROWS = 16
SLOT_OF = (3, 1, 0, 2, 4)
EPSILON = 1e-06
SCALE = 1.0 / math.sqrt(HEAD_DIM)
MASKED = -1e30
TOKENS = 6
MESH = pl.DeviceIdType.MESH


def kernel(
    sizes,
    q_ref, k_ref, v_ref, g_ref, q_gain_ref, k_gain_ref, kv_ref,
    dq_out, dk_out, dv_out, gain_out,
    raw, sent, inv, k_gain, q_gain, gains, bias_own, bias, chain, acc, halo_out, halo_in, back, ret, fin,
    gain_own, gain_plane, gain_z,
    load_sem, fwd_send, fwd_recv, bias_send, bias_recv,
    halo_send, halo_recv, hg_send, hg_recv, ret_send, ret_recv,
    gain_send, gain_recv, token, store_sem,
):
    n_x, n_z, n_dp = sizes
    n_seq = n_x * n_z * RING
    seq = lax.axis_index("seq")
    dp = lax.axis_index("dp")
    me = lax.rem(seq, RING)
    row = seq // RING
    x = lax.rem(row, n_x)
    z = row // n_x

    across = lax.rem(dp + n_dp // 2, n_dp)

    def ring(t):
        return (row * RING + t, dp)

    def over(t):
        return (row * RING + t, across)

    def side(s):
        step = n_seq - RING if s == 0 else RING
        return (lax.rem(seq + step, n_seq), dp)

    def at_plane(t):
        return ((z * n_x + lax.rem(t, n_x)) * RING + me, t // n_x)

    def at_z(t):
        return ((t * n_x + x) * RING + me, dp)

    def ahead(d):
        return lax.rem(me + d, RING)

    def behind(d):
        return lax.rem(me + RING - d, RING)

    def head_cols(home, h):
        return pl.ds(pl.multiple_of((home * HOME + h) * HEAD_DIM, HEAD_DIM), HEAD_DIM)

    def chain_rows(block, count=1):
        return pl.ds(pl.multiple_of((block + 2) * BLOCK, BLOCK), count * BLOCK)

    loads = [
        pltpu.make_async_copy(k_ref, raw.at[0], load_sem.at[0]),
        pltpu.make_async_copy(q_ref, raw.at[1], load_sem.at[1]),
        pltpu.make_async_copy(g_ref, sent.at[0], load_sem.at[2]),
        pltpu.make_async_copy(v_ref, sent.at[1], load_sem.at[3]),
        pltpu.make_async_copy(k_gain_ref, k_gain, load_sem.at[4]),
        pltpu.make_async_copy(q_gain_ref, q_gain, load_sem.at[5]),
    ]
    for load in loads:
        load.start()

    partners = [over(t) for t in range(RING)]
    partners += [ring(ahead(d)) for d in range(1, RING)]
    plane = dp * n_x + x
    partners += [at_plane(lax.rem(plane + d, n_dp * n_x)) for d in range(1, n_dp * n_x)]
    has_side = (row > 0, row < n_x * n_z - 1)
    edges = [(has_side[0], side(0)), (has_side[1], side(1))]
    edges += [(z > 0, at_z(z - 1)), (z < n_z - 1, at_z(z + 1))]
    barrier = pltpu.get_barrier_semaphore()
    for partner in partners:
        pl.semaphore_signal(barrier, 1, device_id=partner, device_id_type=MESH)
    for there, partner in edges:

        @pl.when(there)
        def _(partner=partner):
            pl.semaphore_signal(barrier, 1, device_id=partner, device_id_type=MESH)

    @pl.when(row == 0)
    def _():
        for h in range(HOME):
            chain[h, 1:3, : 2 * BLOCK, :] = jnp.zeros((2, 2 * BLOCK, HEAD_DIM), jnp.bfloat16)
            halo_in[h, 0] = jnp.zeros((2, 2 * BLOCK, HEAD_DIM), jnp.bfloat16)

    @pl.when(row == n_x * n_z - 1)
    def _():
        for h in range(HOME):
            chain[h, 1:3, (RING + 2) * BLOCK :, :] = jnp.zeros((2, 2 * BLOCK, HEAD_DIM), jnp.bfloat16)
            halo_in[h, 1] = jnp.zeros((2, 2 * BLOCK, HEAD_DIM), jnp.bfloat16)

    loads[4].wait()
    loads[5].wait()
    gains[0] = k_gain[...].reshape(1, WIDTH)
    gains[1] = q_gain[...].reshape(1, WIDTH)

    def normed(which):
        def step(i, carry):
            rows = pl.ds(pl.multiple_of(i * ROWS, ROWS), ROWS)
            value = raw[which, rows, :].astype(jnp.float32)
            mean = jnp.sum(value * value, axis=-1, keepdims=True) * (1.0 / WIDTH)
            scale = lax.rsqrt(mean + EPSILON)
            inv[which, rows, :] = jnp.broadcast_to(scale, (ROWS, HEAD_DIM))
            sent[2 + which, rows, :] = (value * scale * gains[which]).astype(jnp.bfloat16)
            return carry

        lax.fori_loop(0, BLOCK // ROWS, step, 0)

    bias_own[...] = jnp.zeros((8, HEAD_DIM), jnp.float32)
    for w in range(WINDOW):
        level = jnp.where(kv_ref[0, SLOT_OF[w]] >= 0, 0.0, MASKED).astype(jnp.float32)
        bias_own[w : w + 1, :] = jnp.full((1, HEAD_DIM), level, jnp.float32)

    def bias_copy(d):
        return pltpu.make_async_remote_copy(
            bias_own, bias.at[me], bias_send.at[d], bias_recv.at[d],
            device_id=over(ahead(d)), device_id_type=MESH,
        )

    def bias_arrival(d):
        return pltpu.make_async_remote_copy(
            bias_own, bias.at[behind(d)], bias_send.at[d], bias_recv.at[d],
            device_id=over(ahead(d)), device_id_type=MESH,
        )

    def forward(h, d, g):
        home = ahead(d)
        part = pl.ds(2 * g, 2)
        return pltpu.make_async_remote_copy(
            sent.at[part, :, head_cols(home, h)], chain.at[h, part, chain_rows(me), :],
            fwd_send.at[h, d, g], fwd_recv.at[h, d, g],
            device_id=over(home), device_id_type=MESH,
        )

    def arrival(h, d, g):
        target = chain.at[h, pl.ds(2 * g, 2), chain_rows(behind(d)), :]
        return pltpu.make_async_remote_copy(
            target, target, fwd_send.at[h, d, g], fwd_recv.at[h, d, g],
            device_id=over(ahead(d)), device_id_type=MESH,
        )

    def halo(h, s):
        mine = pl.ds((2 if s == 0 else RING) * BLOCK, 2 * BLOCK)
        theirs = pl.ds((RING + 2 if s == 0 else 0) * BLOCK, 2 * BLOCK)
        return pltpu.make_async_remote_copy(
            chain.at[h, 1:3, mine, :], chain.at[h, 1:3, theirs, :], halo_send.at[h, s], halo_recv.at[h, s],
            device_id=side(s), device_id_type=MESH,
        )

    def halo_back(h, s):
        return pltpu.make_async_remote_copy(
            halo_out.at[h, s], halo_in.at[h, 1 - s], hg_send.at[h, s], hg_recv.at[h, s],
            device_id=side(s), device_id_type=MESH,
        )

    def target_of(t, home, h):
        cols = head_cols(home, h)
        return ret.at[:, :, cols] if t == 0 else dv_out.at[:, cols]

    def give_back(h, d, t):
        home = ahead(d)
        return pltpu.make_async_remote_copy(
            back.at[h, home, 0:2] if t == 0 else back.at[h, home, 2], target_of(t, me, h),
            ret_send.at[h, d, t], ret_recv.at[h, d, t],
            device_id=over(home), device_id_type=MESH,
        )

    def given(h, d, t):
        target = target_of(t, behind(d), h)
        return pltpu.make_async_remote_copy(
            target, target, ret_send.at[h, d, t], ret_recv.at[h, d, t],
            device_id=over(ahead(d)), device_id_type=MESH,
        )

    loads[0].wait()
    normed(0)
    loads[1].wait()
    normed(1)
    loads[2].wait()
    loads[3].wait()
    n_rows = n_x * n_z
    n_edges = (row + n_rows - 1) // n_rows + (2 * n_rows - 2 - row) // n_rows
    n_edges = n_edges + (z + n_z - 1) // n_z + (2 * n_z - 2 - z) // n_z
    pl.semaphore_wait(barrier, len(partners) + n_edges)

    def tell(r):
        for way in range(2):

            @pl.when((z < n_z - 1) if way else (z > 0))
            def _(way=way):
                pl.semaphore_signal(
                    token.at[way, r], 1, device_id=at_z(z + (1 if way else -1)), device_id_type=MESH
                )

    def hear(r):
        for way in range(2):

            @pl.when((z > 0) if way else (z < n_z - 1))
            def _(way=way):
                pl.semaphore_wait(token.at[way, r], 1)

    def sent_by(s, copy, act):
        @pl.when(has_side[s])
        def _():
            getattr(copy, act)()

    def got_from(s, copy):
        @pl.when(has_side[1 - s])
        def _():
            copy.wait_recv()

    def send_head(h, carry):
        for g in range(2):
            for d in range(RING):
                forward(h, d, g).start()
        return carry

    tell(0)
    send_head(0, 0)
    for d in range(RING):
        bias_copy(d).start()
    send_head(1, 0)

    factor = SCALE * math.log2(math.e)
    by_row = (((1,), (1,)), ((), ()))
    by_col = (((0,), (0,)), ((), ()))

    def return_head(h, t):
        for d in range(RING):
            give_back(h, d, t).start()

    def receive(h):
        for g in range(2):
            for d in range(RING):
                arrival(h, d, g).wait_recv()
        for s in range(2):
            sent_by(s, halo(h, s), "start")

    def work(h):
        acc[...] = jnp.zeros_like(acc)
        for s in range(2):
            got_from(s, halo(h, s))
        gain_q = jnp.zeros((1, HEAD_DIM), jnp.float32)
        for b in range(RING):
            span = slice(b * BLOCK, (b + WINDOW) * BLOCK)
            mine = slice((b + 2) * BLOCK, (b + 3) * BLOCK)
            vals = chain[h, 1, span, :]
            keys = chain[h, 2, span, :]
            grad = chain[h, 0, mine, :]
            query = chain[h, 3, mine, :]
            level = bias[b][:WINDOW].reshape(WINDOW, 1, HEAD_DIM)
            score = lax.dot_general(keys, query, by_row, preferred_element_type=jnp.float32)
            score = score.reshape(WINDOW, BLOCK, HEAD_DIM) * factor + level
            score = score.reshape(WINDOW * BLOCK, HEAD_DIM)
            top = jnp.max(score, axis=0, keepdims=True)
            weight = jnp.exp2(score - top)
            prob = weight * (1.0 / jnp.sum(weight, axis=0, keepdims=True))
            d_prob = lax.dot_general(vals, grad, by_row, preferred_element_type=jnp.float32)
            delta = jnp.sum(prob * d_prob, axis=0, keepdims=True)
            d_score = (prob * (d_prob - delta)).astype(jnp.bfloat16)
            acc[0, span, :] += jnp.dot(d_score, query, preferred_element_type=jnp.float32)
            acc[1, span, :] += jnp.dot(
                prob.astype(jnp.bfloat16), grad, preferred_element_type=jnp.float32
            )
            d_query = lax.dot_general(d_score, keys, by_col, preferred_element_type=jnp.float32) * SCALE
            back[h, b, 0] = d_query.astype(jnp.bfloat16)
            gain_q += jnp.sum(d_query * query.astype(jnp.float32), axis=0, keepdims=True)
        gain_k = jnp.zeros((1, HEAD_DIM), jnp.float32)
        for c in range(CHAIN):
            part = slice(c * BLOCK, (c + 1) * BLOCK)
            gain_k += jnp.sum(acc[0, part, :] * chain[h, 2, part, :].astype(jnp.float32), axis=0, keepdims=True)
        for s in range(2):
            part = slice(0, 2 * BLOCK) if s == 0 else slice((RING + 2) * BLOCK, CHAIN * BLOCK)
            halo_out[h, s, 0] = (acc[0, part, :] * SCALE).astype(jnp.bfloat16)
            halo_out[h, s, 1] = acc[1, part, :].astype(jnp.bfloat16)
            sent_by(s, halo_back(h, s), "start")
        gain_own[pl.ds(h, 1), :] = gain_q / gains[1, :, head_cols(me, h)]
        gain_own[pl.ds(h + 8, 1), :] = gain_k * SCALE / gains[0, :, head_cols(me, h)]

    def settle(h):
        for s in range(2):
            got_from(s, halo_back(h, s))
        for b in range(RING):
            part = slice((b + 2) * BLOCK, (b + 3) * BLOCK)
            came = slice((b % 2) * BLOCK, (b % 2 + 1) * BLOCK)
            for t in range(2):
                extra = halo_in[h, b // 2, t, came, :].astype(jnp.float32)
                own_part = acc[t, part, :]
                if t == 0:
                    own_part = own_part * SCALE
                back[h, b, t + 1] = (own_part + extra).astype(jnp.bfloat16)

    gain_own[...] = jnp.zeros_like(gain_own)

    last = HOME - 1
    receive(0)
    send_head(2, 0)
    for d in range(RING):
        bias_arrival(d).wait_recv()
    work(0)

    def middle(h, carry):
        receive(h)
        hear(2 * h - 2)
        tell(2 * h - 1)

        @pl.when(h + 2 < HOME)
        def _():
            send_head(h + 2, 0)

        settle(h - 1)
        return_head(h - 1, 0)
        work(h)
        hear(2 * h - 1)

        @pl.when(2 * h < TOKENS)
        def _():
            tell(2 * h)

        return carry

    lax.fori_loop(1, last, middle, 0)
    receive(last)
    settle(last - 1)
    return_head(last - 1, 0)
    work(last)

    gain_stages = (
        (gain_plane, plane, n_dp * n_x, at_plane, 0),
        (gain_z, z, n_z, at_z, n_dp * n_x),
        (fin, me, RING, ring, n_dp * n_x + n_z),
    )

    def gain_copy(stage, d, mine):
        slots, place, count, device, base = gain_stages[stage]
        slot = slots.at[place if mine else lax.rem(place + count - d, count)]
        return pltpu.make_async_remote_copy(
            slot, slot, gain_send.at[base + d], gain_recv.at[base + d],
            device_id=device(lax.rem(place + d, count)), device_id_type=MESH,
        )

    def gain_start(stage, value):
        slots, place, count = gain_stages[stage][:3]
        slots[place] = value
        for d in range(1, count):
            gain_copy(stage, d, True).start()

    def gain_finish(stage):
        slots, count = gain_stages[stage][0], gain_stages[stage][2]
        for d in range(1, count):
            gain_copy(stage, d, False).wait_recv()
        total = slots[0]
        for t in range(1, count):
            total = total + slots[t]
        return total

    gain_start(0, gain_own[...])
    settle(last)
    return_head(last, 0)
    for h in range(HOME):
        return_head(h, 1)
    n_tokens = n_seq * BLOCK * n_dp
    gain_start(1, gain_finish(0))
    gain_start(2, gain_finish(1) * (1.0 / math.sqrt(n_tokens)))

    def await_returns(t):
        def step(h, carry):
            for d in range(RING):
                given(h, d, t).wait_recv()
            return carry

        lax.fori_loop(0, HOME, step, 0)

    await_returns(0)

    def finish(which, out_ref):
        def step(i, carry):
            rows = pl.ds(pl.multiple_of(i * ROWS, ROWS), ROWS)
            value = raw[1 - which, rows, :].astype(jnp.float32)
            scaled = gains[1 - which] * ret[which, rows, :].astype(jnp.float32)
            mean = jnp.sum(scaled * value, axis=-1, keepdims=True) * (1.0 / WIDTH)
            scale = inv[1 - which, rows, :][:, :1]
            ret[which, rows, :] = (scale * scaled - value * (scale * scale * scale * mean)).astype(jnp.bfloat16)
            return carry

        lax.fori_loop(0, BLOCK // ROWS, step, 0)
        store = pltpu.make_async_copy(ret.at[which], out_ref, store_sem.at[which])
        store.start()
        return store

    stores = [finish(0, dq_out), finish(1, dk_out)]
    gain_finish(2)
    stores.append(pltpu.make_async_copy(fin, gain_out, store_sem.at[2]))
    stores[2].start()
    await_returns(1)
    for store in stores:
        store.wait()

    for d in range(RING):
        bias_copy(d).wait_send()

    def drain(h, carry):
        for d in range(RING):
            for g in range(2):
                forward(h, d, g).wait_send()
                give_back(h, d, g).wait_send()
        for s in range(2):
            sent_by(s, halo(h, s), "wait_send")
            sent_by(s, halo_back(h, s), "wait_send")
        return carry

    lax.fori_loop(0, HOME, drain, 0)
    for stage in range(3):
        for d in range(1, gain_stages[stage][2]):
            gain_copy(stage, d, True).wait_send()


def hand_over(
    dq_ref, dk_ref, dv_ref, gain_ref, dq_out, dk_out, dv_out, q_out, k_out, held, gains, q_sum, k_sum, in_sem, out_sem
):
    def copy(src, dst, sem, i):
        return pltpu.make_async_copy(src, dst, sem.at[i])

    loads = [copy(gain_ref, gains, in_sem, 0)]
    loads += [copy(src, held.at[i], in_sem, i + 1) for i, src in enumerate((dq_ref, dk_ref, dv_ref))]
    stores = [copy(held.at[i], dst, out_sem, i) for i, dst in enumerate((dq_out, dk_out, dv_out))]
    for load in loads:
        load.start()
    loads[0].wait()
    for home in range(RING):
        for h in range(HOME):
            cols = pl.ds((home * HOME + h) * HEAD_DIM, HEAD_DIM)
            q_sum[cols] = gains[home, h]
            k_sum[cols] = gains[home, 8 + h]
    for load, store in zip(loads[1:], stores):
        load.wait()
        store.start()
    stores += [copy(q_sum, q_out, out_sem, 3), copy(k_sum, k_out, out_sem, 4)]
    for store in stores[3:]:
        store.start()
    for store in stores:
        store.wait()


def body(sizes, q_raw, k_raw, values, d_attn, q_gain, k_gain, kv_lists):
    n_x, n_z, n_dp = sizes
    flat = (BLOCK, WIDTH)
    half = jnp.bfloat16
    anywhere = pl.BlockSpec(memory_space=pl.ANY)
    dma = pltpu.SemaphoreType.DMA
    n_gain = n_dp * n_x + n_z + RING
    pair = (2, 2 * BLOCK, HEAD_DIM)
    d_q, d_k, d_v, gains = pl.pallas_call(
        functools.partial(kernel, sizes),
        out_shape=(
            jax.ShapeDtypeStruct(flat, half),
            jax.ShapeDtypeStruct(flat, half),
            jax.ShapeDtypeStruct(flat, half),
            jax.ShapeDtypeStruct((RING, 16, HEAD_DIM), jnp.float32),
        ),
        in_specs=[anywhere] * 6 + [pl.BlockSpec(memory_space=pltpu.SMEM)],
        out_specs=(anywhere,) * 4,
        scratch_shapes=[
            pltpu.VMEM((2,) + flat, half),
            pltpu.VMEM((4,) + flat, half),
            pltpu.VMEM((2, BLOCK, HEAD_DIM), jnp.float32),
            pltpu.VMEM((WIDTH,), jnp.float32),
            pltpu.VMEM((WIDTH,), jnp.float32),
            pltpu.VMEM((2, 1, WIDTH), jnp.float32),
            pltpu.VMEM((8, HEAD_DIM), jnp.float32),
            pltpu.VMEM((RING, 8, HEAD_DIM), jnp.float32),
            pltpu.VMEM((HOME, 4, CHAIN * BLOCK, HEAD_DIM), half),
            pltpu.VMEM((2, CHAIN * BLOCK, HEAD_DIM), jnp.float32),
            pltpu.VMEM((HOME, 2) + pair, half),
            pltpu.VMEM((HOME, 2) + pair, half),
            pltpu.VMEM((HOME, RING, 3, BLOCK, HEAD_DIM), half),
            pltpu.VMEM((2,) + flat, half),
            pltpu.VMEM((RING, 16, HEAD_DIM), jnp.float32),
            pltpu.VMEM((16, HEAD_DIM), jnp.float32),
            pltpu.VMEM((n_dp * n_x, 16, HEAD_DIM), jnp.float32),
            pltpu.VMEM((n_z, 16, HEAD_DIM), jnp.float32),
            dma((6,)),
            dma((HOME, RING, 2)),
            dma((HOME, RING, 2)),
            dma((RING,)),
            dma((RING,)),
            dma((HOME, 2)),
            dma((HOME, 2)),
            dma((HOME, 2)),
            dma((HOME, 2)),
            dma((HOME, RING, 2)),
            dma((HOME, RING, 2)),
            dma((n_gain,)),
            dma((n_gain,)),
            pltpu.SemaphoreType.REGULAR((2, TOKENS)),
            dma((3,)),
        ],
        compiler_params=pltpu.CompilerParams(
            collective_id=0, has_side_effects=True, vmem_limit_bytes=62 * 1024 * 1024
        ),
    )(
        q_raw.reshape(flat), k_raw.reshape(flat), values.reshape(flat), d_attn.reshape(flat),
        q_gain, k_gain, kv_lists,
    )
    out = pl.pallas_call(
        hand_over,
        out_shape=(jax.ShapeDtypeStruct(flat, half),) * 3 + (jax.ShapeDtypeStruct((WIDTH,), jnp.float32),) * 2,
        in_specs=[anywhere] * 4,
        out_specs=(anywhere,) * 5,
        scratch_shapes=[
            pltpu.VMEM((3,) + flat, half),
            pltpu.VMEM((RING, 16, HEAD_DIM), jnp.float32),
            pltpu.VMEM((WIDTH,), jnp.float32),
            pltpu.VMEM((WIDTH,), jnp.float32),
            dma((4,)),
            dma((5,)),
        ],
    )(d_q, d_k, d_v, gains)
    shape = q_raw.shape
    return tuple(part.reshape(shape) for part in out[:3]) + out[3:]


def solution(mesh):
    rows = mesh.shape["seq"] // RING
    n_x = 4 if rows % 4 == 0 and rows > 4 else 2
    sizes = (n_x, rows // n_x, mesh.shape["dp"])
    split = P("dp", "seq", None)
    return jax.shard_map(
        functools.partial(body, sizes),
        mesh=mesh,
        in_specs=(split, split, split, split, P(), P(), P("seq", None)),
        out_specs=(split, split, split, P(), P()),
        check_vma=False,
    )
```
